512 devices in a mesh: slab: 64 (over z, y), plane: 8 (over x, core).
Axes of the slice: x: 4, y: 8, z: 8, core: 2. Of those that a mesh axis runs over, the one named last changes fastest.
Arguments:
- density: float32 [2, 16, 512, 8192], P(None, 'plane', None, 'slab'), may hold values from -14 to 14
- green: float32 [16, 512, 8192], P('plane', 'slab'), may hold values from -2.5 to -0.15
Outputs:
- potential: float32 [2, 16, 512, 8192], P(None, 'plane', None, 'slab')
- energy: float32 [512], P('slab')
The draws below stay inside these ranges and needn't reach their ends.
All inputs are finite; a program needn't handle non-finite values.
Results may differ from the reference program's by a relative error of at most 0.00013.
Values sent between devices are 32-bit elements; how exact they have to be, the bound alone decides.
No kernel may reach another device: no remote copies, remote signals or barrier semaphores. Data moves between devices by JAX's collectives and lax.ppermute only.
A program may use at most 64 MiB of HBM per device.

```python
import math
import jax
import jax.numpy as jnp
from jax import lax

NX = 8192
NY = 512
B = 16


def draw_density(key, part):
    key = jax.random.fold_in(key, 11)
    first, second = jax.random.split(key)
    base = jnp.clip(jax.random.normal(first, (2, B, NY, NX), jnp.float32), -5.0, 5.0)
    scale = jnp.exp(jax.random.uniform(second, (NY, 1), jnp.float32, math.log(0.5), math.log(2.0)))
    return (base * scale).astype(jnp.float32)


def draw_green(key, part):
    key = jax.random.fold_in(key, 23)
    planes = jnp.arange(B, dtype=jnp.float32)[:, None, None]
    rising = jnp.power(3.0, planes / max(B - 1, 1))
    rough = jnp.exp(jax.random.uniform(key, (B, NY, NX), jnp.float32, -0.7, 0.7))
    values = -0.4 * rough * rising
    return values.astype(jnp.float32)


def setup_inputs(seed: int = 0) -> dict:
    streams_of = jax.random.split(jax.random.key(seed), 3)
    return {
        "density": draw_density(jax.random.fold_in(streams_of[2], 71), 0),
        "green": draw_green(jax.random.fold_in(streams_of[2], 71), 0),
    }


def reference(density, green):
    def one_plane(items):
        part_real, part_imag, kernel = items
        spectrum = jnp.fft.fft(lax.complex(part_real, part_imag), axis=-1)
        power = jnp.sum(kernel * (jnp.real(spectrum) ** 2 + jnp.imag(spectrum) ** 2), axis=-1)
        back = jnp.fft.ifft(spectrum * kernel, axis=-1)
        return jnp.real(back), jnp.imag(back), power

    out_real, out_imag, power = lax.map(one_plane, (density[0], density[1], green))
    energy = jnp.sum(power, axis=0) / (NX * NX * B)
    potential = jnp.stack([out_real, out_imag]).astype(jnp.float32)
    return potential, energy.astype(jnp.float32)
```

```python
import math

import numpy as np
import ml_dtypes

import jax
import jax.numpy as jnp
from jax import lax
from jax.experimental import pallas as pl
from jax.experimental.pallas import tpu as pltpu
from jax.sharding import PartitionSpec as P


def split_constant(table):
    high = table.astype(np.float32).astype(ml_dtypes.bfloat16)
    low = (table - high.astype(np.float64)).astype(np.float32).astype(ml_dtypes.bfloat16)
    return high, low


def waves(rows, cols, size):
    product = np.outer(np.arange(rows), np.arange(cols)) % size
    angle = 2.0 * math.pi / size * product
    return np.cos(angle), np.sin(angle)


def constant_tables(outer, inner):
    length = outer * inner
    cos_o, sin_o = waves(outer, outer, outer)
    mix = np.zeros((2, outer, outer, 2))
    mix[0, :, :, 0] = cos_o
    mix[0, :, :, 1] = sin_o
    mix[1, :, :, 0] = -sin_o
    mix[1, :, :, 1] = cos_o
    forward = mix.reshape(2 * outer, 2 * outer)
    unmix = np.zeros((outer, 2, 2, outer))
    unmix[:, 0, 0, :] = cos_o
    unmix[:, 0, 1, :] = -sin_o
    unmix[:, 1, 0, :] = sin_o
    unmix[:, 1, 1, :] = cos_o
    inverse = unmix.reshape(2 * outer, 2 * outer) / length
    cos_i, sin_i = waves(inner, inner, inner)
    spread = np.block([[cos_i, -sin_i], [sin_i, cos_i]])
    gather = np.block([[cos_i, sin_i], [-sin_i, cos_i]])
    tables = []
    for matrix in (forward, inverse):
        high, low = split_constant(matrix)
        tables.append(np.block([[high, high], [low, low]]))
    for matrix in (spread, gather):
        tables.extend(split_constant(matrix))
    cos_t, sin_t = waves(outer, inner, length)
    tables.append(cos_t.astype(np.float32))
    tables.append(sin_t.astype(np.float32))
    return tables


def halves(value):
    high = value.astype(jnp.bfloat16)
    low = (value - high.astype(jnp.float32)).astype(jnp.bfloat16)
    return high, low


def matmul(left, right):
    return jnp.dot(left, right, preferred_element_type=jnp.float32)


def line_kernel(
    lines_ref, green_ref, fwd_ref, inv_ref, sp_hi, sp_lo, ga_hi, ga_lo, cos_ref, sin_ref,
    out_ref, energy_ref,
):
    outer, inner = cos_ref.shape
    count = green_ref.shape[0] // outer
    rows = 2 * outer
    cos_t, sin_t = cos_ref[...], sin_ref[...]
    pair_count = 2
    for first in range(0, count, pair_count):
        group = range(first, first + pair_count)
        block = jnp.concatenate(
            [lines_ref[pl.ds(line, rows, stride=count), :] for line in group], axis=1
        )
        mixed = matmul(fwd_ref[...], jnp.concatenate(halves(block), axis=0))
        mixed = mixed[:rows] + mixed[rows:]
        turned = []
        for n in range(pair_count):
            real = mixed[:outer, n * inner:(n + 1) * inner]
            imag = mixed[outer:, n * inner:(n + 1) * inner]
            turned.append(
                jnp.concatenate(
                    [real * cos_t + imag * sin_t, imag * cos_t - real * sin_t], axis=1
                )
            )
        high, low = halves(jnp.concatenate(turned, axis=0))
        spectrum = matmul(high, sp_hi[...]) + matmul(low, sp_hi[...]) + matmul(high, sp_lo[...])
        real, imag = spectrum[:, :inner], spectrum[:, inner:]
        green = green_ref[first * outer:(first + pair_count) * outer, :]
        weighted_real, weighted_imag = green * real, green * imag
        power = weighted_real * real + weighted_imag * imag
        for n, line in enumerate(group):
            energy_ref[line:line + 1, :] = jnp.sum(
                power[n * outer:(n + 1) * outer], axis=0, keepdims=True
            )
        high, low = halves(jnp.concatenate([weighted_real, weighted_imag], axis=1))
        back = matmul(high, ga_hi[...]) + matmul(low, ga_hi[...]) + matmul(high, ga_lo[...])
        stacked = []
        for n in range(pair_count):
            real = back[n * outer:(n + 1) * outer, :inner]
            imag = back[n * outer:(n + 1) * outer, inner:]
            stacked.append(
                jnp.concatenate(
                    [real * cos_t - imag * sin_t, imag * cos_t + real * sin_t], axis=0
                )
            )
        block = jnp.concatenate(stacked, axis=1)
        result = matmul(inv_ref[...], jnp.concatenate(halves(block), axis=0))
        result = result[:rows] + result[rows:]
        for n, line in enumerate(group):
            out_ref[pl.ds(line, rows, stride=count), :] = result[:, n * inner:(n + 1) * inner]


def convolve_lines(lines, green, tables):
    vmem = pl.BlockSpec(memory_space=pltpu.VMEM)
    count = green.shape[0] // tables[-1].shape[0]
    return pl.pallas_call(
        line_kernel,
        out_shape=(
            jax.ShapeDtypeStruct(lines.shape, jnp.float32),
            jax.ShapeDtypeStruct((count, lines.shape[1]), jnp.float32),
        ),
        in_specs=[vmem] * (2 + len(tables)),
        out_specs=(vmem, vmem),
        compiler_params=pltpu.CompilerParams(vmem_limit_bytes=24 * 1024 * 1024),
        cost_estimate=pl.CostEstimate(
            flops=16 * 10 * 256**3 * 2, bytes_accessed=4 * 1024 * 1024, transcendentals=0
        ),
    )(lines, green, *tables)


def shards(density, green):
    slab_count = lax.axis_size("slab")
    parts, plane_local, lines_all, local_x = density.shape
    length = local_x * slab_count
    planes_all = plane_local * lax.axis_size("plane")
    line_local = lines_all // slab_count
    tables = [jnp.asarray(t) for t in constant_tables(slab_count, local_x)]
    tiles = density.reshape(parts, plane_local, slab_count, line_local, local_x)
    sent = jnp.transpose(tiles, (2, 0, 1, 3, 4))
    moved = lax.all_to_all(sent, "slab", split_axis=0, concat_axis=0, tiled=True)
    kernels = jnp.swapaxes(green.reshape(plane_local, line_local, local_x, slab_count), 2, 3)
    result, energy = convolve_lines(
        moved.reshape(slab_count * parts * plane_local * line_local, local_x),
        kernels.reshape(plane_local * line_local * slab_count, local_x),
        tables,
    )
    result = result.reshape(slab_count, parts, plane_local, line_local, local_x)
    returned = lax.all_to_all(result, "slab", split_axis=0, concat_axis=0, tiled=True)
    potential = jnp.transpose(returned, (1, 2, 0, 3, 4)).reshape(density.shape)
    energy = jnp.sum(energy.reshape(plane_local, line_local, local_x), axis=(0, 2))
    energy = lax.psum(energy, "plane") / (length * length * planes_all)
    return (potential, energy)


def solution(mesh):
    placed = (P(None, "plane", None, "slab"), P("plane", "slab", None))
    return jax.shard_map(
        shards,
        mesh=mesh,
        in_specs=placed,
        out_specs=(P(None, "plane", None, "slab"), P("slab")),
        check_vma=False,
    )
```

```python
import math

import numpy as np
import ml_dtypes

import jax
import jax.numpy as jnp
from jax import lax
from jax.experimental import pallas as pl
from jax.experimental.pallas import tpu as pltpu
from jax.sharding import PartitionSpec as P


def split_constant(table):
    high = table.astype(np.float32).astype(ml_dtypes.bfloat16)
    low = (table - high.astype(np.float64)).astype(np.float32).astype(ml_dtypes.bfloat16)
    return high, low


def waves(rows, cols, size):
    product = np.outer(rows, cols) % size
    angle = 2.0 * math.pi / size * product
    return np.cos(angle), np.sin(angle)


def constant_tables(outer, inner):
    length = outer * inner
    natural, line = np.arange(outer), np.arange(inner)
    halved = np.concatenate([line[0::2], line[1::2]])
    cos_o, sin_o = waves(natural, natural, outer)
    mix = np.stack(
        [np.stack([cos_o, sin_o], axis=2), np.stack([-sin_o, cos_o], axis=2)], axis=0
    ).reshape(2 * outer, 2 * outer)
    unmix = mix.T / length
    cos_i, sin_i = waves(line, halved, inner)
    spread = np.block([[cos_i, -sin_i], [sin_i, cos_i]])
    tables = []
    for matrix in (mix, unmix):
        high, low = split_constant(matrix)
        tables.append(np.block([[high, high], [low, low]]))
    for matrix in (spread, spread.T):
        high, low = split_constant(matrix)
        tables.append(np.concatenate([high, high, low], axis=0))
    cos_t, sin_t = waves(natural, line, length)
    return tables + [cos_t.astype(np.float32), sin_t.astype(np.float32)]


def halves(value):
    high = value.astype(jnp.bfloat16)
    low = (value - high.astype(jnp.float32)).astype(jnp.bfloat16)
    return high, low


def matmul(left, right):
    return jnp.dot(left, right, preferred_element_type=jnp.float32)


def spread_rows(value, table_ref):
    high, low = halves(value)
    return matmul(jnp.concatenate([high, low, high], axis=1), table_ref[...])


def mix_lines(lines, table_ref):
    block = jnp.concatenate(lines, axis=1)
    product = matmul(table_ref[...], jnp.concatenate(halves(block), axis=0))
    rows = product.shape[0] // 2
    return product[:rows] + product[rows:]


def line_kernel(
    lines_ref, green_ref, mix_ref, unmix_ref, spread_ref, gather_ref, cos_ref, sin_ref,
    out_ref, energy_ref,
):
    outer, inner = cos_ref.shape
    rows = 2 * outer
    planes, _, per_plane, _ = green_ref.shape
    count = planes * per_plane
    pair = 2
    cos_t, sin_t = cos_ref[...], sin_ref[...]
    turned = []
    for first in range(0, count, pair):
        mixed = mix_lines(
            [lines_ref[pl.ds(first + n, rows, stride=count), :] for n in range(pair)], mix_ref
        )
        for n in range(pair):
            real = mixed[:outer, n * inner:(n + 1) * inner]
            imag = mixed[outer:, n * inner:(n + 1) * inner]
            turned.append(
                jnp.concatenate(
                    [real * cos_t + imag * sin_t, imag * cos_t - real * sin_t], axis=1
                )
            )
    spectrum = spread_rows(jnp.concatenate(turned, axis=0), spread_ref)
    weighted = []
    for line in range(count):
        green = green_ref[line // per_plane, :, line % per_plane, :].T
        green = jnp.concatenate([green[:outer], green[outer:]], axis=1)
        real = spectrum[line * outer:(line + 1) * outer, :inner]
        imag = spectrum[line * outer:(line + 1) * outer, inner:]
        green_real, green_imag = green * real, green * imag
        energy_ref[line:line + 1, :] = jnp.sum(
            green_real * real + green_imag * imag, axis=0, keepdims=True
        )
        weighted.append(jnp.concatenate([green_real, green_imag], axis=1))
    back = spread_rows(jnp.concatenate(weighted, axis=0), gather_ref)
    for first in range(0, count, pair):
        turned = []
        for line in range(first, first + pair):
            real = back[line * outer:(line + 1) * outer, :inner]
            imag = back[line * outer:(line + 1) * outer, inner:]
            turned.append(
                jnp.concatenate(
                    [real * cos_t - imag * sin_t, imag * cos_t + real * sin_t], axis=0
                )
            )
        result = mix_lines(turned, unmix_ref)
        for n in range(pair):
            out_ref[pl.ds(first + n, rows, stride=count), :] = result[:, n * inner:(n + 1) * inner]


def convolve_lines(lines, green, tables):
    vmem = pl.BlockSpec(memory_space=pltpu.VMEM)
    count = green.shape[0] * green.shape[2]
    return pl.pallas_call(
        line_kernel,
        out_shape=(
            jax.ShapeDtypeStruct(lines.shape, jnp.float32),
            jax.ShapeDtypeStruct((count, lines.shape[1]), jnp.float32),
        ),
        in_specs=[vmem] * (2 + len(tables)),
        out_specs=(vmem, vmem),
        compiler_params=pltpu.CompilerParams(vmem_limit_bytes=40 * 1024 * 1024),
        cost_estimate=pl.CostEstimate(
            flops=16 * 10 * 256**3, bytes_accessed=4 * 1024 * 1024, transcendentals=0
        ),
    )(lines, green, *tables)


def shards(density, green):
    slab_count = lax.axis_size("slab")
    parts, plane_local, lines_all, local_x = density.shape
    length = local_x * slab_count
    planes_all = plane_local * lax.axis_size("plane")
    line_local = lines_all // slab_count
    tables = [jnp.asarray(t) for t in constant_tables(slab_count, local_x)]
    tiles = density.reshape(parts, plane_local, slab_count, line_local, local_x)
    sent = jnp.transpose(tiles, (2, 0, 1, 3, 4))
    moved = lax.all_to_all(sent, "slab", split_axis=0, concat_axis=0, tiled=True)
    by_line = green.reshape(plane_local, line_local, slab_count, local_x)
    result, energy = convolve_lines(
        moved.reshape(slab_count * parts * plane_local * line_local, local_x),
        jnp.transpose(by_line, (0, 2, 1, 3)),
        tables,
    )
    result = result.reshape(slab_count, parts, plane_local, line_local, local_x)
    returned = lax.all_to_all(result, "slab", split_axis=0, concat_axis=0, tiled=True)
    potential = jnp.transpose(returned, (1, 2, 0, 3, 4)).reshape(density.shape)
    energy = jnp.sum(energy.reshape(plane_local, line_local, local_x), axis=(0, 2))
    energy = lax.psum(energy, "plane") / (length * length * planes_all)
    return (potential, energy)


def solution(mesh):
    placed = (P(None, "plane", None, "slab"), P("plane", "slab", None))
    return jax.shard_map(
        shards,
        mesh=mesh,
        in_specs=placed,
        out_specs=(P(None, "plane", None, "slab"), P("slab")),
        check_vma=False,
    )
```

```python
from functools import partial
import math

import numpy as np
import ml_dtypes

import jax
import jax.numpy as jnp
from jax import lax
from jax.experimental import pallas as pl
from jax.experimental.pallas import tpu as pltpu
from jax.sharding import PartitionSpec as P


def split_constant(table):
    high = table.astype(np.float32).astype(ml_dtypes.bfloat16)
    low = (table - high.astype(np.float64)).astype(np.float32).astype(ml_dtypes.bfloat16)
    return high, low


def waves(rows, cols, size):
    product = np.outer(rows, cols) % size
    angle = 2.0 * math.pi / size * product
    return np.cos(angle), np.sin(angle)


def constant_tables(arrival, departure, inner):
    outer = len(arrival)
    length = outer * inner
    natural, line = np.arange(outer), np.arange(inner)
    halved = np.concatenate([line[0::2], line[1::2]])
    mixes = []
    for order in (arrival, departure):
        cos_o, sin_o = waves(natural, order, outer)
        mix = np.stack(
            [np.stack([cos_o, sin_o], axis=2), np.stack([-sin_o, cos_o], axis=2)], axis=0
        )
        mixes.append(mix.reshape(2 * outer, 2 * outer))
    cos_i, sin_i = waves(line, halved, inner)
    spread = np.block([[cos_i, -sin_i], [sin_i, cos_i]])
    tables = []
    for matrix in (mixes[0], mixes[1].T / length):
        high, low = split_constant(matrix)
        tables.append(np.block([[high, high], [low, low]]))
    for matrix in (spread, spread.T):
        high, low = split_constant(matrix)
        tables.append(np.concatenate([high, high, low], axis=0))
    cos_t, sin_t = waves(natural, line, length)
    return tables + [cos_t.astype(np.float32), sin_t.astype(np.float32)]


def halves(value):
    high = value.astype(jnp.bfloat16)
    low = (value - high.astype(jnp.float32)).astype(jnp.bfloat16)
    return high, low


def matmul(left, right):
    return jnp.dot(left, right, preferred_element_type=jnp.float32)


def spread_rows(value, table_ref):
    high, low = halves(value)
    return matmul(jnp.concatenate([high, low, high], axis=1), table_ref[...])


def mix_lines(lines, table_ref):
    block = jnp.concatenate(lines, axis=1)
    product = matmul(table_ref[...], jnp.concatenate(halves(block), axis=0))
    rows = product.shape[0] // 2
    return product[:rows] + product[rows:]


def line_kernel(
    lines_ref, green_ref, mix_ref, unmix_ref, spread_ref, gather_ref, cos_ref, sin_ref,
    out_ref, energy_ref,
):
    outer, inner = cos_ref.shape
    rows = 2 * outer
    planes, _, per_plane, _ = green_ref.shape
    count = planes * per_plane
    pair = 2
    cos_t, sin_t = cos_ref[...], sin_ref[...]
    turned = []
    for first in range(0, count, pair):
        mixed = mix_lines(
            [lines_ref[pl.ds(first + n, rows, stride=count), :] for n in range(pair)], mix_ref
        )
        for n in range(pair):
            real = mixed[:outer, n * inner:(n + 1) * inner]
            imag = mixed[outer:, n * inner:(n + 1) * inner]
            turned.append(
                jnp.concatenate(
                    [real * cos_t + imag * sin_t, imag * cos_t - real * sin_t], axis=1
                )
            )
    spectrum = spread_rows(jnp.concatenate(turned, axis=0), spread_ref)
    weighted = []
    for line in range(count):
        green = green_ref[line // per_plane, :, line % per_plane, :].T
        green = jnp.concatenate([green[:outer], green[outer:]], axis=1)
        real = spectrum[line * outer:(line + 1) * outer, :inner]
        imag = spectrum[line * outer:(line + 1) * outer, inner:]
        green_real, green_imag = green * real, green * imag
        energy_ref[line:line + 1, :] = jnp.sum(
            green_real * real + green_imag * imag, axis=0, keepdims=True
        )
        weighted.append(jnp.concatenate([green_real, green_imag], axis=1))
    back = spread_rows(jnp.concatenate(weighted, axis=0), gather_ref)
    for first in range(0, count, pair):
        turned = []
        for line in range(first, first + pair):
            real = back[line * outer:(line + 1) * outer, :inner]
            imag = back[line * outer:(line + 1) * outer, inner:]
            turned.append(
                jnp.concatenate(
                    [real * cos_t - imag * sin_t, imag * cos_t + real * sin_t], axis=0
                )
            )
        result = mix_lines(turned, unmix_ref)
        for n in range(pair):
            out_ref[pl.ds(first + n, rows, stride=count), :] = result[:, n * inner:(n + 1) * inner]


def convolve_lines(lines, green, tables):
    vmem = pl.BlockSpec(memory_space=pltpu.VMEM)
    count = green.shape[0] * green.shape[2]
    return pl.pallas_call(
        line_kernel,
        out_shape=(
            jax.ShapeDtypeStruct(lines.shape, jnp.float32),
            jax.ShapeDtypeStruct((count, lines.shape[1]), jnp.float32),
        ),
        in_specs=[vmem] * (2 + len(tables)),
        out_specs=(vmem, vmem),
        compiler_params=pltpu.CompilerParams(vmem_limit_bytes=40 * 1024 * 1024),
        cost_estimate=pl.CostEstimate(
            flops=16 * 10 * 256**3, bytes_accessed=4 * 1024 * 1024, transcendentals=0
        ),
    )(lines, green, *tables)


def shards(density, green):
    slab_count, plane_count = lax.axis_size("slab"), lax.axis_size("plane")
    parts, plane_local, lines_all, local_x = density.shape
    length = local_x * slab_count
    planes_all = plane_local * plane_count
    line_local = lines_all // slab_count
    first = slab_count - 5 * slab_count // 16
    order = np.roll(np.arange(slab_count), -first)
    groups = [
        [int(slab) * plane_count + plane for slab in order] for plane in range(plane_count)
    ]
    exchange = partial(
        lax.all_to_all,
        axis_name=("slab", "plane"),
        split_axis=0,
        concat_axis=0,
        axis_index_groups=groups,
        tiled=True,
    )
    tables = [jnp.asarray(t) for t in constant_tables(order, order, local_x)]
    tiles = density.reshape(parts, plane_local, slab_count, line_local, local_x)
    sent = jnp.transpose(tiles, (2, 0, 1, 3, 4))
    sent = jnp.concatenate([sent[first:], sent[:first]], axis=0)
    moved = exchange(sent)
    by_line = green.reshape(plane_local, line_local, slab_count, local_x)
    result, energy = convolve_lines(
        moved.reshape(slab_count * parts * plane_local * line_local, local_x),
        jnp.transpose(by_line, (0, 2, 1, 3)),
        tables,
    )
    returned = exchange(result.reshape(sent.shape))
    returned = jnp.concatenate([returned[slab_count - first:], returned[:slab_count - first]], axis=0)
    potential = jnp.transpose(returned, (1, 2, 0, 3, 4)).reshape(density.shape)
    energy = jnp.sum(energy.reshape(plane_local, line_local, local_x), axis=(0, 2))
    energy = lax.psum(energy, "plane") / (length * length * planes_all)
    return (potential, energy)


def solution(mesh):
    placed = (P(None, "plane", None, "slab"), P("plane", "slab", None))
    return jax.shard_map(
        shards,
        mesh=mesh,
        in_specs=placed,
        out_specs=(P(None, "plane", None, "slab"), P("slab")),
        check_vma=False,
    )
```

```python
from functools import partial
import math

import numpy as np
import ml_dtypes

import jax
import jax.numpy as jnp
from jax import lax
from jax.experimental import pallas as pl
from jax.experimental.pallas import tpu as pltpu
from jax.sharding import PartitionSpec as P


def split_constant(table):
    high = table.astype(np.float32).astype(ml_dtypes.bfloat16)
    low = (table - high.astype(np.float64)).astype(np.float32).astype(ml_dtypes.bfloat16)
    return high, low


def waves(rows, cols, size):
    product = np.outer(rows, cols) % size
    angle = 2.0 * math.pi / size * product
    return np.cos(angle), np.sin(angle)


def constant_tables(arrival, departure, inner):
    outer = len(arrival)
    length = outer * inner
    natural, line = np.arange(outer), np.arange(inner)
    halved = np.concatenate([line[0::2], line[1::2]])
    mixes = []
    for order in (arrival, departure):
        cos_o, sin_o = waves(natural, order, outer)
        mix = np.stack(
            [np.stack([cos_o, sin_o], axis=2), np.stack([-sin_o, cos_o], axis=2)], axis=0
        )
        mixes.append(mix.reshape(2 * outer, 2 * outer))
    cos_i, sin_i = waves(line, halved, inner)
    spread = np.block([[cos_i, -sin_i], [sin_i, cos_i]])
    tables = []
    for matrix in (mixes[0], mixes[1].T / length):
        high, low = split_constant(matrix)
        tables.append(np.block([[high, high], [low, low]]))
    for matrix in (spread, spread.T):
        high, low = split_constant(matrix)
        tables.append(np.concatenate([high, high, low], axis=0))
    cos_t, sin_t = waves(natural, line, length)
    return tables + [cos_t.astype(np.float32), sin_t.astype(np.float32)]


def halves(value):
    high = value.astype(jnp.bfloat16)
    low = (value - high.astype(jnp.float32)).astype(jnp.bfloat16)
    return high, low


def matmul(left, right):
    return jnp.dot(left, right, preferred_element_type=jnp.float32)


def spread_rows(value, table_ref):
    high, low = halves(value)
    return matmul(jnp.concatenate([high, low, high], axis=1), table_ref[...])


def mix_lines(lines, table_ref):
    block = jnp.concatenate(lines, axis=1)
    product = matmul(table_ref[...], jnp.concatenate(halves(block), axis=0))
    rows = product.shape[0] // 2
    return product[:rows] + product[rows:]


def line_kernel(
    lines_ref, green_ref, mix_ref, unmix_ref, spread_ref, gather_ref, cos_ref, sin_ref,
    out_ref, energy_ref,
):
    outer, inner = cos_ref.shape
    rows = 2 * outer
    planes, _, per_plane, _ = green_ref.shape
    count = planes * per_plane
    pair = 2
    cos_t, sin_t = cos_ref[...], sin_ref[...]
    def enter(first, size):
        turned = []
        for line in range(first, first + size, pair):
            mixed = mix_lines(
                [lines_ref[pl.ds(line + n, rows, stride=count), :] for n in range(pair)], mix_ref
            )
            for n in range(pair):
                real = mixed[:outer, n * inner:(n + 1) * inner]
                imag = mixed[outer:, n * inner:(n + 1) * inner]
                turned.append(
                    jnp.concatenate(
                        [real * cos_t + imag * sin_t, imag * cos_t - real * sin_t], axis=1
                    )
                )
        return jnp.concatenate(turned, axis=0)

    def weigh(first, size, spectrum):
        weighted = []
        for n in range(size):
            line = first + n
            green = green_ref[line // per_plane, :, line % per_plane, :].T
            green = jnp.concatenate([green[:outer], green[outer:]], axis=1)
            real = spectrum[n * outer:(n + 1) * outer, :inner]
            imag = spectrum[n * outer:(n + 1) * outer, inner:]
            green_real, green_imag = green * real, green * imag
            energy_ref[line:line + 1, :] = jnp.sum(
                green_real * real + green_imag * imag, axis=0, keepdims=True
            )
            weighted.append(jnp.concatenate([green_real, green_imag], axis=1))
        return jnp.concatenate(weighted, axis=0)

    def leave(first, size, back):
        for start in range(0, size, pair):
            turned = []
            for n in range(start, start + pair):
                real = back[n * outer:(n + 1) * outer, :inner]
                imag = back[n * outer:(n + 1) * outer, inner:]
                turned.append(
                    jnp.concatenate(
                        [real * cos_t - imag * sin_t, imag * cos_t + real * sin_t], axis=0
                    )
                )
            result = mix_lines(turned, unmix_ref)
            for n in range(pair):
                line = first + start + n
                out_ref[pl.ds(line, rows, stride=count), :] = result[:, n * inner:(n + 1) * inner]

    groups = 2
    size = count // groups
    state = {}
    stages = [
        lambda g: enter(g * size, size),
        lambda g: spread_rows(state[g], spread_ref),
        lambda g: weigh(g * size, size, state[g]),
        lambda g: spread_rows(state[g], gather_ref),
        lambda g: leave(g * size, size, state[g]),
    ]
    for wave in range(groups + len(stages) - 1):
        for stage, run in enumerate(stages):
            group = wave - stage
            if 0 <= group < groups:
                state[group] = run(group)


def convolve_lines(lines, green, tables):
    vmem = pl.BlockSpec(memory_space=pltpu.VMEM)
    count = green.shape[0] * green.shape[2]
    return pl.pallas_call(
        line_kernel,
        out_shape=(
            jax.ShapeDtypeStruct(lines.shape, jnp.float32),
            jax.ShapeDtypeStruct((count, lines.shape[1]), jnp.float32),
        ),
        in_specs=[vmem] * (2 + len(tables)),
        out_specs=(vmem, vmem),
        compiler_params=pltpu.CompilerParams(vmem_limit_bytes=40 * 1024 * 1024),
        cost_estimate=pl.CostEstimate(
            flops=16 * 10 * 256**3, bytes_accessed=4 * 1024 * 1024, transcendentals=0
        ),
    )(lines, green, *tables)


def shards(density, green):
    slab_count, plane_count = lax.axis_size("slab"), lax.axis_size("plane")
    parts, plane_local, lines_all, local_x = density.shape
    length = local_x * slab_count
    planes_all = plane_local * plane_count
    line_local = lines_all // slab_count
    first = slab_count - 5 * slab_count // 16
    order = np.roll(np.arange(slab_count), -first)
    groups = [
        [int(slab) * plane_count + plane for slab in order] for plane in range(plane_count)
    ]
    exchange = partial(
        lax.all_to_all,
        axis_name=("slab", "plane"),
        split_axis=0,
        concat_axis=0,
        axis_index_groups=groups,
        tiled=True,
    )
    tables = [jnp.asarray(t) for t in constant_tables(order, order, local_x)]
    tiles = density.reshape(parts, plane_local, slab_count, line_local, local_x)
    sent = jnp.transpose(tiles, (2, 0, 1, 3, 4))
    sent = jnp.concatenate([sent[first:], sent[:first]], axis=0)
    moved = exchange(sent)
    by_line = green.reshape(plane_local, line_local, slab_count, local_x)
    result, energy = convolve_lines(
        moved.reshape(slab_count * parts * plane_local * line_local, local_x),
        jnp.transpose(by_line, (0, 2, 1, 3)),
        tables,
    )
    returned = exchange(result.reshape(sent.shape))
    returned = jnp.concatenate([returned[slab_count - first:], returned[:slab_count - first]], axis=0)
    potential = jnp.transpose(returned, (1, 2, 0, 3, 4)).reshape(density.shape)
    energy = jnp.sum(energy.reshape(plane_local, line_local, local_x), axis=(0, 2))
    energy = lax.psum(energy, "plane") / (length * length * planes_all)
    return (potential, energy)


def solution(mesh):
    placed = (P(None, "plane", None, "slab"), P("plane", "slab", None))
    return jax.shard_map(
        shards,
        mesh=mesh,
        in_specs=placed,
        out_specs=(P(None, "plane", None, "slab"), P("slab")),
        check_vma=False,
    )
```

```python
from functools import partial
import math

import numpy as np
import ml_dtypes

import jax
import jax.numpy as jnp
from jax import lax
from jax.experimental import pallas as pl
from jax.experimental.pallas import tpu as pltpu
from jax.sharding import PartitionSpec as P


def split_constant(table):
    high = table.astype(np.float32).astype(ml_dtypes.bfloat16)
    low = (table - high.astype(np.float64)).astype(np.float32).astype(ml_dtypes.bfloat16)
    return high, low


def waves(rows, cols, size):
    product = np.outer(rows, cols) % size
    angle = 2.0 * math.pi / size * product
    return np.cos(angle), np.sin(angle)


def constant_tables(arrival, departure, inner):
    outer = len(arrival)
    length = outer * inner
    natural, line = np.arange(outer), np.arange(inner)
    halved = np.concatenate([line[0::2], line[1::2]])
    mixes = []
    for order in (arrival, departure):
        cos_o, sin_o = waves(natural, order, outer)
        mix = np.stack(
            [np.stack([cos_o, sin_o], axis=2), np.stack([-sin_o, cos_o], axis=2)], axis=0
        )
        mixes.append(mix.reshape(2 * outer, 2 * outer))
    cos_i, sin_i = waves(line, halved, inner)
    spread = np.block([[cos_i, -sin_i], [sin_i, cos_i]])
    tables = []
    for matrix in (mixes[0], mixes[1].T / length):
        high, low = split_constant(matrix)
        tables.append(np.block([[high, high], [low, low]]))
    for matrix in (spread, spread.T):
        high, low = split_constant(matrix)
        tables.append(np.concatenate([high, high, low], axis=0))
    cos_t, sin_t = waves(natural, line, length)
    return tables + [cos_t.astype(np.float32), sin_t.astype(np.float32)]


def halves(value):
    high = value.astype(jnp.bfloat16)
    low = (value - high.astype(jnp.float32)).astype(jnp.bfloat16)
    return high, low


def matmul(left, right):
    return jnp.dot(left, right, preferred_element_type=jnp.float32)


def spread_rows(value, table_ref):
    high, low = halves(value)
    return matmul(jnp.concatenate([high, low, high], axis=1), table_ref[...])


def mix_lines(lines, table_ref):
    block = jnp.concatenate(lines, axis=1)
    product = matmul(table_ref[...], jnp.concatenate(halves(block), axis=0))
    rows = product.shape[0] // 2
    return product[:rows] + product[rows:]


def line_kernel(
    lines_ref, green_ref, mix_ref, unmix_ref, spread_ref, gather_ref, cos_ref, sin_ref,
    out_ref, energy_ref,
):
    outer, inner = cos_ref.shape
    rows = 2 * outer
    planes, _, per_plane, _ = green_ref.shape
    count = planes * per_plane
    pair = 2
    cos_t, sin_t = cos_ref[...], sin_ref[...]

    def enter(first, size):
        turned = []
        for line in range(first, first + size, pair):
            mixed = mix_lines(
                [lines_ref[pl.ds(line + n, rows, stride=count), :] for n in range(pair)], mix_ref
            )
            for n in range(pair):
                real = mixed[:outer, n * inner:(n + 1) * inner]
                imag = mixed[outer:, n * inner:(n + 1) * inner]
                turned.append(
                    jnp.concatenate(
                        [real * cos_t + imag * sin_t, imag * cos_t - real * sin_t], axis=1
                    )
                )
        return jnp.concatenate(turned, axis=0)

    def weigh(first, size, spectrum):
        weighted = []
        for n in range(size):
            line = first + n
            green = green_ref[line // per_plane, :, line % per_plane, :].T
            green = jnp.concatenate([green[:outer], green[outer:]], axis=1)
            real = spectrum[n * outer:(n + 1) * outer, :inner]
            imag = spectrum[n * outer:(n + 1) * outer, inner:]
            green_real, green_imag = green * real, green * imag
            energy_ref[line:line + 1, :] = jnp.sum(
                green_real * real + green_imag * imag, axis=0, keepdims=True
            )
            weighted.append(jnp.concatenate([green_real, green_imag], axis=1))
        return jnp.concatenate(weighted, axis=0)

    def leave(first, size, back):
        for start in range(0, size, pair):
            turned = []
            for n in range(start, start + pair):
                real = back[n * outer:(n + 1) * outer, :inner]
                imag = back[n * outer:(n + 1) * outer, inner:]
                turned.append(
                    jnp.concatenate(
                        [real * cos_t - imag * sin_t, imag * cos_t + real * sin_t], axis=0
                    )
                )
            result = mix_lines(turned, unmix_ref)
            for n in range(pair):
                line = first + start + n
                out_ref[pl.ds(line, rows, stride=count), :] = result[:, n * inner:(n + 1) * inner]

    groups = 2
    size = count // groups
    state = {}
    stages = [
        lambda g: enter(g * size, size),
        lambda g: spread_rows(state[g], spread_ref),
        lambda g: weigh(g * size, size, state[g]),
        lambda g: spread_rows(state[g], gather_ref),
        lambda g: leave(g * size, size, state[g]),
    ]
    for wave in range(groups + len(stages) - 1):
        for stage, run in enumerate(stages):
            group = wave - stage
            if 0 <= group < groups:
                state[group] = run(group)


def convolve_lines(lines, green, tables):
    vmem = pl.BlockSpec(memory_space=pltpu.VMEM)
    count = green.shape[0] * green.shape[2]
    return pl.pallas_call(
        line_kernel,
        out_shape=(
            jax.ShapeDtypeStruct(lines.shape, jnp.float32),
            jax.ShapeDtypeStruct((count, lines.shape[1]), jnp.float32),
        ),
        in_specs=[vmem] * (2 + len(tables)),
        out_specs=(vmem, vmem),
        compiler_params=pltpu.CompilerParams(vmem_limit_bytes=40 * 1024 * 1024),
        cost_estimate=pl.CostEstimate(
            flops=16 * 10 * 256**3, bytes_accessed=4 * 1024 * 1024, transcendentals=0
        ),
    )(lines, green, *tables)


def pack_messages(tiles, order):
    def kernel(tiles_ref, sent_ref):
        for rank, slab in enumerate(order):
            sent_ref[rank] = tiles_ref[int(slab)]

    vmem = pl.BlockSpec(memory_space=pltpu.VMEM)
    return pl.pallas_call(
        kernel,
        out_shape=jax.ShapeDtypeStruct(tiles.shape, tiles.dtype),
        in_specs=[vmem],
        out_specs=vmem,
        compiler_params=pltpu.CompilerParams(vmem_limit_bytes=8 * 1024 * 1024),
    )(tiles)


def unpack_messages(returned, order):
    slabs, parts, planes, *tile = returned.shape
    shape = (parts, planes, slabs, *tile)

    def kernel(returned_ref, out_ref, staged, sems):
        copies = []
        for part in range(parts):
            for plane in range(planes):
                for rank, slab in enumerate(order):
                    staged[part, plane, int(slab)] = returned_ref[rank, part, plane]
                copies.append(
                    pltpu.make_async_copy(
                        staged.at[part, plane], out_ref.at[part, plane], sems.at[part, plane]
                    )
                )
                copies[-1].start()
        for copy in copies:
            copy.wait()

    return pl.pallas_call(
        kernel,
        out_shape=jax.ShapeDtypeStruct(shape, returned.dtype),
        in_specs=[pl.BlockSpec(memory_space=pltpu.VMEM)],
        out_specs=pl.BlockSpec(memory_space=pl.ANY),
        scratch_shapes=[
            pltpu.VMEM(shape, returned.dtype),
            pltpu.SemaphoreType.DMA((parts, planes)),
        ],
        compiler_params=pltpu.CompilerParams(vmem_limit_bytes=8 * 1024 * 1024),
    )(returned)


def shards(density, green):
    slab_count, plane_count = lax.axis_size("slab"), lax.axis_size("plane")
    parts, plane_local, lines_all, local_x = density.shape
    length = local_x * slab_count
    planes_all = plane_local * plane_count
    line_local = lines_all // slab_count
    first = slab_count - 5 * slab_count // 16
    order = np.roll(np.arange(slab_count), -first)
    groups = [
        [int(slab) * plane_count + plane for slab in order] for plane in range(plane_count)
    ]
    exchange = partial(
        lax.all_to_all,
        axis_name=("slab", "plane"),
        split_axis=0,
        concat_axis=0,
        axis_index_groups=groups,
        tiled=True,
    )
    tables = [jnp.asarray(t) for t in constant_tables(order, order, local_x)]
    tiles = density.reshape(parts, plane_local, slab_count, line_local, local_x)
    sent = jnp.transpose(tiles, (2, 0, 1, 3, 4))
    sent = pack_messages(sent, order)
    moved = exchange(sent)
    by_line = green.reshape(plane_local, line_local, slab_count, local_x)
    result, energy = convolve_lines(
        moved.reshape(slab_count * parts * plane_local * line_local, local_x),
        jnp.transpose(by_line, (0, 2, 1, 3)),
        tables,
    )
    returned = exchange(result.reshape(sent.shape))
    potential = unpack_messages(returned, order).reshape(density.shape)
    energy = jnp.sum(energy.reshape(plane_local, line_local, local_x), axis=(0, 2))
    energy = lax.psum(energy, "plane") / (length * length * planes_all)
    return (potential, energy)


def solution(mesh):
    placed = (P(None, "plane", None, "slab"), P("plane", "slab", None))
    return jax.shard_map(
        shards,
        mesh=mesh,
        in_specs=placed,
        out_specs=(P(None, "plane", None, "slab"), P("slab")),
        check_vma=False,
    )
```

```python
from functools import partial
import math

import numpy as np
import ml_dtypes

import jax
import jax.numpy as jnp
from jax import lax
from jax.experimental import pallas as pl
from jax.experimental.pallas import tpu as pltpu
from jax.sharding import PartitionSpec as P


def split_constant(table):
    high = table.astype(np.float32).astype(ml_dtypes.bfloat16)
    low = (table - high.astype(np.float64)).astype(np.float32).astype(ml_dtypes.bfloat16)
    return high, low


def waves(rows, cols, size):
    product = np.outer(rows, cols) % size
    angle = 2.0 * math.pi / size * product
    return np.cos(angle), np.sin(angle)


def constant_tables(arrival, departure, inner):
    outer = len(arrival)
    length = outer * inner
    natural, line = np.arange(outer), np.arange(inner)
    halved = np.concatenate([line[0::2], line[1::2]])
    mixes = []
    for order in (arrival, departure):
        cos_o, sin_o = waves(natural, order, outer)
        mix = np.stack(
            [np.stack([cos_o, sin_o], axis=2), np.stack([-sin_o, cos_o], axis=2)], axis=0
        )
        mixes.append(mix.reshape(2 * outer, 2 * outer))
    cos_i, sin_i = waves(line, halved, inner)
    spread = np.block([[cos_i, -sin_i], [sin_i, cos_i]])
    tables = []
    for matrix in (mixes[0], mixes[1].T / length):
        high, low = split_constant(matrix)
        tables.append(np.block([[high, high], [low, low]]))
    for matrix in (spread, spread.T):
        high, low = split_constant(matrix)
        tables.append(np.concatenate([high, high, low], axis=0))
    cos_t, sin_t = waves(natural, line, length)
    return tables + [cos_t.astype(np.float32), sin_t.astype(np.float32)]


def halves(value):
    high = value.astype(jnp.bfloat16)
    low = (value - high.astype(jnp.float32)).astype(jnp.bfloat16)
    return high, low


def matmul(left, right):
    return jnp.dot(left, right, preferred_element_type=jnp.float32)


def spread_rows(value, table_ref):
    high, low = halves(value)
    return matmul(jnp.concatenate([high, low, high], axis=1), table_ref[...])


def mix_lines(lines, table_ref):
    block = jnp.concatenate(lines, axis=1)
    product = matmul(table_ref[...], jnp.concatenate(halves(block), axis=0))
    rows = product.shape[0] // 2
    return product[:rows] + product[rows:]


def line_kernel(
    lines_ref, green_ref, mix_ref, unmix_ref, spread_ref, gather_ref, cos_ref, sin_ref,
    out_ref, energy_ref,
):
    outer, inner = cos_ref.shape
    rows = 2 * outer
    planes, _, per_plane, _ = green_ref.shape
    count = planes * per_plane
    pair = 8
    cos_t, sin_t = cos_ref[...], sin_ref[...]

    def enter(first, size):
        turned = []
        for line in range(first, first + size, pair):
            mixed = mix_lines(
                [lines_ref[pl.ds(line + n, rows, stride=count), :] for n in range(pair)], mix_ref
            )
            for n in range(pair):
                real = mixed[:outer, n * inner:(n + 1) * inner]
                imag = mixed[outer:, n * inner:(n + 1) * inner]
                turned.append(
                    jnp.concatenate(
                        [real * cos_t + imag * sin_t, imag * cos_t - real * sin_t], axis=1
                    )
                )
        return jnp.concatenate(turned, axis=0)

    def weigh(first, size, spectrum):
        weighted = []
        for n in range(size):
            line = first + n
            green = green_ref[line // per_plane, :, line % per_plane, :].T
            green = jnp.concatenate([green[:outer], green[outer:]], axis=1)
            real = spectrum[n * outer:(n + 1) * outer, :inner]
            imag = spectrum[n * outer:(n + 1) * outer, inner:]
            green_real, green_imag = green * real, green * imag
            energy_ref[line:line + 1, :] = jnp.sum(
                green_real * real + green_imag * imag, axis=0, keepdims=True
            )
            weighted.append(jnp.concatenate([green_real, green_imag], axis=1))
        return jnp.concatenate(weighted, axis=0)

    def leave(first, size, back):
        for start in range(0, size, pair):
            turned = []
            for n in range(start, start + pair):
                real = back[n * outer:(n + 1) * outer, :inner]
                imag = back[n * outer:(n + 1) * outer, inner:]
                turned.append(
                    jnp.concatenate(
                        [real * cos_t - imag * sin_t, imag * cos_t + real * sin_t], axis=0
                    )
                )
            result = mix_lines(turned, unmix_ref)
            for n in range(pair):
                line = first + start + n
                out_ref[pl.ds(line, rows, stride=count), :] = result[:, n * inner:(n + 1) * inner]

    groups = 2
    size = count // groups
    state = {}
    stages = [
        lambda g: enter(g * size, size),
        lambda g: spread_rows(state[g], spread_ref),
        lambda g: weigh(g * size, size, state[g]),
        lambda g: spread_rows(state[g], gather_ref),
        lambda g: leave(g * size, size, state[g]),
    ]
    for wave in range(groups + len(stages) - 1):
        for stage, run in enumerate(stages):
            group = wave - stage
            if 0 <= group < groups:
                state[group] = run(group)


def convolve_lines(lines, green, tables):
    vmem = pl.BlockSpec(memory_space=pltpu.VMEM)
    count = green.shape[0] * green.shape[2]
    return pl.pallas_call(
        line_kernel,
        out_shape=(
            jax.ShapeDtypeStruct(lines.shape, jnp.float32),
            jax.ShapeDtypeStruct((count, lines.shape[1]), jnp.float32),
        ),
        in_specs=[vmem] * (2 + len(tables)),
        out_specs=(vmem, vmem),
        compiler_params=pltpu.CompilerParams(vmem_limit_bytes=40 * 1024 * 1024),
        cost_estimate=pl.CostEstimate(
            flops=16 * 10 * 256**3, bytes_accessed=4 * 1024 * 1024, transcendentals=0
        ),
    )(lines, green, *tables)


def pack_messages(tiles, order):
    def kernel(tiles_ref, sent_ref):
        for rank, slab in enumerate(order):
            sent_ref[rank] = tiles_ref[int(slab)]

    vmem = pl.BlockSpec(memory_space=pltpu.VMEM)
    return pl.pallas_call(
        kernel,
        out_shape=jax.ShapeDtypeStruct(tiles.shape, tiles.dtype),
        in_specs=[vmem],
        out_specs=vmem,
        compiler_params=pltpu.CompilerParams(vmem_limit_bytes=8 * 1024 * 1024),
    )(tiles)


def unpack_messages(returned, order):
    slabs, parts, planes, *tile = returned.shape
    shape = (parts, planes, slabs, *tile)

    def kernel(returned_ref, out_ref, staged, sems):
        copies = []
        for part in range(parts):
            for plane in range(planes):
                for rank, slab in enumerate(order):
                    staged[part, plane, int(slab)] = returned_ref[rank, part, plane]
                copies.append(
                    pltpu.make_async_copy(
                        staged.at[part, plane], out_ref.at[part, plane], sems.at[part, plane]
                    )
                )
                copies[-1].start()
        for copy in copies:
            copy.wait()

    return pl.pallas_call(
        kernel,
        out_shape=jax.ShapeDtypeStruct(shape, returned.dtype),
        in_specs=[pl.BlockSpec(memory_space=pltpu.VMEM)],
        out_specs=pl.BlockSpec(memory_space=pl.ANY),
        scratch_shapes=[
            pltpu.VMEM(shape, returned.dtype),
            pltpu.SemaphoreType.DMA((parts, planes)),
        ],
        compiler_params=pltpu.CompilerParams(vmem_limit_bytes=8 * 1024 * 1024),
    )(returned)


def shards(density, green):
    slab_count, plane_count = lax.axis_size("slab"), lax.axis_size("plane")
    parts, plane_local, lines_all, local_x = density.shape
    length = local_x * slab_count
    planes_all = plane_local * plane_count
    line_local = lines_all // slab_count
    first = slab_count - 5 * slab_count // 16
    order = np.roll(np.arange(slab_count), -first)
    groups = [
        [int(slab) * plane_count + plane for slab in order] for plane in range(plane_count)
    ]
    exchange = partial(
        lax.all_to_all,
        axis_name=("slab", "plane"),
        split_axis=0,
        concat_axis=0,
        axis_index_groups=groups,
        tiled=True,
    )
    tables = [jnp.asarray(t) for t in constant_tables(order, order, local_x)]
    tiles = density.reshape(parts, plane_local, slab_count, line_local, local_x)
    sent = jnp.transpose(tiles, (2, 0, 1, 3, 4))
    sent = pack_messages(sent, order)
    moved = exchange(sent)
    by_line = green.reshape(plane_local, line_local, slab_count, local_x)
    result, energy = convolve_lines(
        moved.reshape(slab_count * parts * plane_local * line_local, local_x),
        jnp.transpose(by_line, (0, 2, 1, 3)),
        tables,
    )
    returned = exchange(result.reshape(sent.shape))
    potential = unpack_messages(returned, order).reshape(density.shape)
    energy = jnp.sum(energy.reshape(plane_local, line_local, local_x), axis=(0, 2))
    energy = lax.psum(energy, "plane") / (length * length * planes_all)
    return (potential, energy)


def solution(mesh):
    placed = (P(None, "plane", None, "slab"), P("plane", "slab", None))
    return jax.shard_map(
        shards,
        mesh=mesh,
        in_specs=placed,
        out_specs=(P(None, "plane", None, "slab"), P("slab")),
        check_vma=False,
    )
```
